256 devices in a mesh: wide: 128 (over z, y_hi, x, core), narrow: 2 (over y_lo).
Axes of the slice: x: 4, y: 4 (y_hi: 2, y_lo: 2; y = y_hi * 2 + y_lo), z: 8, core: 2. Of those that a mesh axis runs over, the one named last changes fastest.
Arguments:
- tokens: bfloat16 [16384, 4096], P('wide', 'narrow'), may hold values from -6 to 6
- router_weight: bfloat16 [4096, 128], P('narrow'), may hold values from -0.046875 to 0.046875
- route_ids: int32 [16384, 8], P('wide'), may hold values from 0 to 127, as said below
- slot_index: int32 [16384, 8], P('wide'), may hold values from 0 to 11, as said below
- w_gate: bfloat16 [4096, 24576], P('narrow', 'wide'), may hold values from -0.09375 to 0.09375
- w_up: bfloat16 [4096, 24576], P('narrow', 'wide'), may hold values from -0.09375 to 0.09375
- w_down: bfloat16 [24576, 4096], P('wide', 'narrow'), may hold values from -1.25 to 1.25
- cotangent: bfloat16 [16384, 4096], P('wide', 'narrow'), may hold values from -1.5 to 1.5
Outputs:
- layer_out: bfloat16 [16384, 4096], P('wide', 'narrow')
- input_grad: bfloat16 [16384, 4096], P('wide', 'narrow')
- grad_gate: bfloat16 [4096, 24576], P('narrow', 'wide')
- grad_up: bfloat16 [4096, 24576], P('narrow', 'wide')
- grad_down: bfloat16 [24576, 4096], P('wide', 'narrow')
The draws below stay inside these ranges and needn't reach their ends.
Inputs may be any that keep to these rules, and one draw needn't show every extreme that they name: `route_ids`: each row names 8 different experts, and entry k of a row names an expert equal to k modulo 8. Among the rows of one index of wide every expert is named at least twice and at most 12 times, and among the rows of index 0 of wide some expert below 16 is named exactly 12 times. `slot_index`: for each index of wide and each expert, the rows of that index naming the expert hold distinct slots 0 up to their number minus one, in no particular order.
All inputs are finite; a program needn't handle non-finite values.
Results may differ from the reference program's by a relative error of at most 0.015.
Values may be sent and summed in bfloat16 or wider, within the bound.
No kernel may reach another device: no remote copies, remote signals or barrier semaphores. Data moves between devices by JAX's collectives and lax.ppermute only.
A program may use at most 128 MiB of HBM per device.

```python
import jax
import jax.numpy as jnp
from jax import lax

D = 4096
FF = 1536
TOP = 8
EXPERTS_ALL = 128
TOK_DEV = 128
SLICES = 8
WINDOW = 16
FF_DEV = 192
CAP = 12
TOKENS = 16384
N_WIDE = 128


count_profiles = [[12, 12, 11, 11, 10, 10, 9, 9, 8, 8, 7, 6, 5, 4, 3, 3], [12, 11, 11, 10, 10, 10, 9, 9, 8, 8, 7, 6, 6, 5, 4, 2], [12, 12, 12, 10, 9, 9, 9, 8, 8, 7, 7, 7, 6, 5, 4, 3], [12, 10, 10, 10, 10, 9, 9, 9, 8, 8, 8, 7, 6, 5, 4, 3]]


def route_table(key):
    pick_key, order_key, place_key = jax.random.split(key, 3)
    blocks = TOKENS // TOK_DEV
    members = EXPERTS_ALL // TOP
    scale_up = TOK_DEV // 128
    table = jnp.array(count_profiles, dtype=jnp.int32)
    which = jax.random.randint(pick_key, (blocks, TOP), 0, 4)
    counts_base = table[which] * scale_up
    member_iota = jnp.arange(members, dtype=jnp.int32)
    order_scores = jax.random.randint(order_key, (blocks, TOP, members), 0, 2 ** 20) * members + member_iota
    order = jnp.argsort(order_scores, axis=2)
    counts = jnp.take_along_axis(counts_base, order, axis=2)
    first_block = (jnp.arange(blocks) == 0)[:, None, None]
    counts = jnp.where(first_block, counts_base, counts)
    ends = jnp.cumsum(counts, axis=2)
    starts = ends - counts
    token_iota = jnp.arange(TOK_DEV, dtype=jnp.int32)
    place_scores = jax.random.randint(place_key, (blocks, TOP, TOK_DEV), 0, 2 ** 20) * TOK_DEV + token_iota
    position = jnp.argsort(place_scores, axis=2).astype(jnp.int32)
    member = jnp.sum((position[:, :, :, None] >= ends[:, :, None, :]).astype(jnp.int32), axis=3)
    slots = position - jnp.take_along_axis(starts, member, axis=2)
    experts = member * TOP + jnp.arange(TOP, dtype=jnp.int32)[None, :, None]
    experts = experts.transpose(0, 2, 1).reshape(TOKENS, TOP).astype(jnp.int32)
    slots = slots.transpose(0, 2, 1).reshape(TOKENS, TOP).astype(jnp.int32)
    return (experts, slots)


def draw_route_ids(key, part):
    experts, slots = route_table(key)
    return experts


def draw_slot_index(key, part):
    experts, slots = route_table(key)
    return slots


def draw_tokens(key, part):
    key = jax.random.fold_in(key, 11)
    base_key = jax.random.fold_in(key, 0)
    values = jax.random.truncated_normal(base_key, -6.0, 6.0, (TOKENS, D), jnp.float32)
    return values.astype(jnp.bfloat16)


def level_of(stream_key, shape, pieces, smallest, top_value):
    def one(dim, parts):
        heights = jax.random.uniform(jax.random.fold_in(jax.random.fold_in(stream_key, 6), dim), (parts,), jnp.float32, smallest / len(pieces), top_value / len(pieces))
        return jnp.repeat(jnp.exp(heights), shape[dim] // parts).reshape((-1,) + (1,) * (len(shape) - dim - 1))

    level = one(*pieces[0])
    for cut in pieces[1:]:
        level = level * one(*cut)
    return level


def normal_values(own_key, extent, deviation, limit, pieces=(), held_as=jnp.bfloat16):
    entries = deviation * jax.random.normal(own_key, extent, jnp.float32)
    if pieces:
        entries = entries * level_of(own_key, extent, pieces, -0.22, 0.18)
    return jnp.clip(entries, -limit, limit).astype(held_as)


def setup_inputs(seed: int = 0) -> dict:
    arg_keys = jax.random.split(jax.random.key(seed), 9)
    tokens = draw_tokens(jax.random.fold_in(arg_keys[8], 71), 0)
    router_weight = normal_values(arg_keys[1], (D, EXPERTS_ALL), (4 * D) ** -0.5, 0.046875, ((0, 2),))
    route_ids = draw_route_ids(jax.random.fold_in(arg_keys[8], 71), 0)
    slot_index = draw_slot_index(jax.random.fold_in(arg_keys[8], 71), 0)
    w_gate = normal_values(arg_keys[4], (D, WINDOW * FF), D ** -0.5, 0.09375, ((0, 2), (1, 128)))
    w_up = normal_values(arg_keys[5], (D, WINDOW * FF), D ** -0.5, 0.09375, ((0, 2), (1, 128)))
    w_down = normal_values(arg_keys[6], (WINDOW * FF, D), (FF // 64) ** -0.5, 1.25, ((0, 128), (1, 2)))
    cotangent = normal_values(arg_keys[7], (TOKENS, D), 0.25, 1.5, ((0, 128), (1, 2)))
    return {"tokens": tokens, "router_weight": router_weight, "route_ids": route_ids, "slot_index": slot_index, "w_gate": w_gate, "w_up": w_up, "w_down": w_down, "cotangent": cotangent}


def expert_pass(operands):
    rows_in, cot_in, gate_w, up_w, down_w = operands
    gate_pre = jnp.dot(rows_in, gate_w, preferred_element_type=jnp.float32)
    up_pre = jnp.dot(rows_in, up_w, preferred_element_type=jnp.float32)
    hidden = (jax.nn.silu(gate_pre) * up_pre).astype(jnp.bfloat16)
    hidden_sliced = hidden.reshape(-1, SLICES, FF_DEV).astype(jnp.float32)
    down_sliced = down_w.reshape(SLICES, FF_DEV, D).astype(jnp.float32)
    outputs = jnp.einsum("rsf,sfd->srd", hidden_sliced, down_sliced).astype(jnp.bfloat16)
    outputs = lax.optimization_barrier(outputs).astype(jnp.float32)
    expert_out = jnp.sum(outputs, axis=0)
    hidden_grad = jnp.dot(cot_in, down_w.T, preferred_element_type=jnp.float32)
    sigma_gate = jax.nn.sigmoid(gate_pre)
    pre_gate = (hidden_grad * up_pre * sigma_gate * (1.0 + gate_pre * (1.0 - sigma_gate))).astype(jnp.bfloat16)
    pre_up = (hidden_grad * gate_pre * sigma_gate).astype(jnp.bfloat16)
    grad_gate = jnp.dot(rows_in.T, pre_gate, preferred_element_type=jnp.float32).astype(jnp.bfloat16)
    grad_up = jnp.dot(rows_in.T, pre_up, preferred_element_type=jnp.float32).astype(jnp.bfloat16)
    grad_down = jnp.dot(hidden.T, cot_in, preferred_element_type=jnp.float32).astype(jnp.bfloat16)
    gate_sliced = pre_gate.reshape(-1, SLICES, FF_DEV).astype(jnp.float32)
    up_sliced = pre_up.reshape(-1, SLICES, FF_DEV).astype(jnp.float32)
    backs = jnp.einsum("rsf,dsf->srd", gate_sliced, gate_w.reshape(D, SLICES, FF_DEV).astype(jnp.float32))
    backs = backs + jnp.einsum("rsf,dsf->srd", up_sliced, up_w.reshape(D, SLICES, FF_DEV).astype(jnp.float32))
    backs = lax.optimization_barrier(backs.astype(jnp.bfloat16)).astype(jnp.float32)
    expert_back = jnp.sum(backs, axis=0)
    return expert_out, expert_back, grad_gate, grad_up, grad_down


def reference(tokens, router_weight, route_ids, slot_index, w_gate, w_up, w_down, cotangent):
    window = N_WIDE // SLICES
    slot_rows = N_WIDE * CAP
    logits = jnp.dot(tokens, router_weight, preferred_element_type=jnp.float32)
    chosen = jnp.take_along_axis(logits, route_ids, axis=1)
    weights_exp = jnp.exp(chosen)
    gate_share = weights_exp / jnp.sum(weights_exp, axis=1, keepdims=True)
    token_iota = jnp.arange(TOKENS, dtype=jnp.int32)
    block_index = token_iota // TOK_DEV
    inside = route_ids < window
    expert_index = jnp.where(inside, route_ids, window).astype(jnp.int32)
    row_index = (block_index[:, None] * CAP + slot_index).astype(jnp.int32)
    expert_rows = jnp.zeros((window, slot_rows, D), jnp.bfloat16)
    cot_rows = jnp.zeros((window, slot_rows, D), jnp.bfloat16)
    cot_float = cotangent.astype(jnp.float32)
    for route in range(TOP):
        expert_rows = expert_rows.at[expert_index[:, route], row_index[:, route]].set(tokens, mode="drop")
        scaled = (gate_share[:, route:route + 1] * cot_float).astype(jnp.bfloat16)
        cot_rows = cot_rows.at[expert_index[:, route], row_index[:, route]].set(scaled, mode="drop")
    gate_stack = w_gate.reshape(D, window, FF).transpose(1, 0, 2)
    up_stack = w_up.reshape(D, window, FF).transpose(1, 0, 2)
    down_stack = w_down.reshape(window, FF, D)
    expert_out, expert_back, grad_gate, grad_up, grad_down = lax.map(
        expert_pass, (expert_rows, cot_rows, gate_stack, up_stack, down_stack))
    layer_acc = jnp.zeros((TOKENS, D), jnp.float32)
    back_acc = jnp.zeros((TOKENS, D), jnp.float32)
    grads_list = []
    for route in range(TOP):
        safe = jnp.minimum(expert_index[:, route], window - 1).astype(jnp.int32)
        mask = inside[:, route:route + 1]
        picked_out = expert_out[safe, row_index[:, route]]
        layer_acc = layer_acc + jnp.where(mask, gate_share[:, route:route + 1] * picked_out, 0.0)
        grads_list.append(jnp.where(inside[:, route], jnp.sum(cot_float * picked_out, axis=1), 0.0))
        back_acc = back_acc + jnp.where(mask, expert_back[safe, row_index[:, route]], 0.0)
    layer_out = layer_acc.astype(jnp.bfloat16)
    gate_grad = jnp.stack(grads_list, axis=1)
    gate_mean = jnp.sum(gate_share * gate_grad, axis=1, keepdims=True)
    logit_grad = jnp.zeros((TOKENS, EXPERTS_ALL), jnp.float32)
    logit_grad = logit_grad.at[token_iota[:, None], route_ids].set(gate_share * (gate_grad - gate_mean))
    logit_grad = logit_grad.astype(jnp.bfloat16)
    router_back = jnp.dot(logit_grad, router_weight.T, preferred_element_type=jnp.float32)
    input_grad = (back_acc + router_back).astype(jnp.bfloat16)
    grad_gate = grad_gate.transpose(1, 0, 2).reshape(D, window * FF)
    grad_up = grad_up.transpose(1, 0, 2).reshape(D, window * FF)
    grad_down = grad_down.reshape(window * FF, D)
    return (layer_out, input_grad, grad_gate, grad_up, grad_down)
```

```python
import jax
import jax.numpy as jnp
import numpy as np
from jax import lax
from jax.experimental import pallas as pl
from jax.experimental.pallas import tpu as pltpu
from jax.sharding import PartitionSpec as P

CAP = 12
NZ, NYH, NX, NC = 8, 2, 4, 2
BLOCK = 2 * CAP
F32 = jnp.float32
BF16 = jnp.bfloat16


def wide_perm(move):
    pairs = []
    for z in range(NZ):
        for y in range(NYH):
            for x in range(NX):
                for c in range(NC):
                    a, b, d, e = move(z, y, x, c)
                    pairs.append((((z * NYH + y) * NX + x) * NC + c, ((a * NYH + b) * NX + d) * NC + e))
    return pairs


PERM_C = wide_perm(lambda z, y, x, c: (z, y, x, 1 - c))
PERM_X = wide_perm(lambda z, y, x, c: (z, y, x ^ 1, c))
PERM_W = wide_perm(lambda z, y, x, c: (z, y, NX - 1 - x, c))
PERM_Y = wide_perm(lambda z, y, x, c: (z, 1 - y, x, c))
PERM_Z = [wide_perm(lambda z, y, x, c, k=k: ((z + k) % NZ, y, x, c)) for k in range(NZ)]
FAR_FIRST = (4, 3, 5, 2, 6, 1, 7)


def swap_c(v):
    return lax.ppermute(v, "wide", PERM_C)


def swap_x(v):
    return lax.ppermute(v, "wide", PERM_X)


def swap_w(v):
    return lax.ppermute(v, "wide", PERM_W)


def swap_y(v):
    return lax.ppermute(v, "wide", PERM_Y)


def swap_n(v):
    return lax.ppermute(v, "narrow", [(0, 1), (1, 0)])


def dot(a, b, dims, out=F32):
    return lax.dot_general(a, b, (dims, ((), ())), preferred_element_type=out)


NN = ((1,), (0,))
NT = ((1,), (1,))
TN = ((0,), (0,))


VMEM = pl.BlockSpec(memory_space=pltpu.VMEM)
ANY = pl.BlockSpec(memory_space=pl.ANY)
PARAMS = pltpu.CompilerParams(vmem_limit_bytes=16 * 2**20)


def merge(pieces, after=()):
    count = len(pieces)
    rows = [p.shape[0] for p in pieces]
    starts = [sum(rows[:i]) for i in range(count)]

    def kernel(*refs):
        out = refs[-1]
        for i in range(count):
            out[pl.ds(starts[i], rows[i]), :] = refs[i][...]

    return pl.pallas_call(
        kernel,
        out_shape=jax.ShapeDtypeStruct((sum(rows),) + pieces[0].shape[1:], pieces[0].dtype),
        in_specs=[VMEM] * count + [ANY] * len(after),
        out_specs=VMEM,
        compiler_params=PARAMS,
    )(*pieces, *after)


def reorder(pieces, order, sizes, after=()):
    count = len(pieces)
    starts = [sum(sizes[:i]) for i in range(len(sizes))]
    select = jnp.asarray(order[:, None] == np.arange(len(order))[None, :], BF16)

    def kernel(select_ref, *refs):
        ins, outs = refs[:count], refs[count + len(after) :]
        rows = jnp.concatenate([r[...].astype(F32) for r in ins], axis=0).astype(BF16)
        for start, out in zip(starts, outs):
            picked = dot(select_ref[pl.ds(start, out.shape[0]), :], rows, NN)
            out[...] = picked.astype(BF16)

    return pl.pallas_call(
        kernel,
        out_shape=[jax.ShapeDtypeStruct((size, pieces[0].shape[1]), BF16) for size in sizes],
        in_specs=[VMEM] * (1 + count) + [ANY] * len(after),
        out_specs=[VMEM] * len(sizes),
        compiler_params=PARAMS,
    )(select, *pieces, *after)


ROW = np.arange(NZ * CAP)
SPLIT = np.concatenate([ROW // CAP * BLOCK + ROW % CAP, ROW // CAP * BLOCK + ROW % CAP + CAP])
JOIN = np.argsort(SPLIT)


def along_z(rows):
    blocks = [rows[k * BLOCK : (k + 1) * BLOCK] for k in range(NZ)]
    got = [blocks[0]] + [None] * (NZ - 1)
    for k in FAR_FIRST:
        got[k] = lax.ppermute(blocks[k], "wide", PERM_Z[k])
    return got


def split_y(got, after=()):
    return reorder(got, SPLIT, [NZ * CAP] * 2, after)


def spread(keep, give):
    near = swap_x(keep)
    other = swap_y(give)
    far = swap_x(other)
    mine = [keep, other, near, far]
    return mine + [swap_c(m) for m in mine]


def total_x(low, high):
    from_c = swap_c(high)
    quarter = low.shape[0] // 2
    sent = swap_x((low[quarter:].astype(F32) + from_c[quarter:].astype(F32)).astype(BF16))
    return (low[:quarter].astype(F32) + from_c[:quarter].astype(F32) + sent.astype(F32)).astype(BF16)


def join_y(total):
    eighth = total.shape[0] // 2
    keep = total[:eighth]
    other = swap_y(total[eighth:])
    return reorder([keep, other], JOIN, [BLOCK] * NZ)


def back_z(blocks):
    got = [blocks[0]] + [None] * (NZ - 1)
    for k in FAR_FIRST:
        got[k] = lax.ppermute(blocks[k], "wide", PERM_Z[NZ - k])
    return jnp.concatenate(got, axis=0)


def local(tokens, router_weight, route_ids, slot_index, w_gate, w_up, w_down, cotangent):
    width = w_gate.shape[1]
    place = lax.axis_index("wide")
    my_z = place // (NYH * NX * NC)
    my_y = (place // (NX * NC)) % NYH

    own_gu = jnp.concatenate([w_gate, w_up], axis=1)
    par_gu = swap_w(own_gu)
    par_down = swap_w(w_down)

    slots = NZ * BLOCK
    shift = (route_ids // NYH - my_z) % NZ
    flip = (route_ids % NYH) ^ my_y
    column = jnp.where(route_ids < NZ * NYH, shift * BLOCK + flip * CAP + slot_index, -1)
    slot_iota = lax.broadcasted_iota(jnp.int32, (1, 1, slots), 2)
    placed = (column[:, :, None] == slot_iota).astype(F32)
    occupied = jnp.sum(placed, axis=1).astype(BF16)
    got_rows = along_z(dot(occupied, tokens, TN).astype(BF16))

    logits_part = jnp.dot(tokens, router_weight, preferred_element_type=F32)
    logits = logits_part + swap_n(logits_part)
    expert_iota = lax.broadcasted_iota(jnp.int32, (1, 1, router_weight.shape[1]), 2)
    picked = (route_ids[:, :, None] == expert_iota).astype(F32)
    chosen = jnp.sum(picked * logits[:, None, :], axis=2)
    weights_exp = jnp.exp(chosen)
    gate_share = weights_exp / jnp.sum(weights_exp, axis=1, keepdims=True)
    weighted = jnp.sum(placed * gate_share[:, :, None], axis=1)
    row_share = jnp.sum(weighted, axis=0)[:, None]
    send_cot = (dot(occupied, cotangent, TN) * row_share).astype(BF16)

    row_parts = spread(*split_y(got_rows, (send_cot,)))
    got_cot = along_z(send_cot)
    keep_cot, give_cot = split_y(got_cot)
    rows_in = merge(row_parts, after=(keep_cot, give_cot, par_gu))
    cot_parts = spread(keep_cot, give_cot)

    own_part = dot(rows_in, own_gu, NN)
    par_part = dot(rows_in, par_gu, NN)
    own = own_part + swap_n(own_part.astype(BF16)).astype(F32)
    par = par_part + swap_n(par_part.astype(BF16)).astype(F32)
    cot_in = merge(cot_parts, after=(own_part, par_part))
    down = merge([w_down, par_down])
    hidden_part = dot(cot_in, down, NT)
    hidden_grad = hidden_part + swap_n(hidden_part.astype(BF16)).astype(F32)

    gate_pre = jnp.concatenate([own[:, :width], par[:, :width]], axis=1)
    up_pre = jnp.concatenate([own[:, width:], par[:, width:]], axis=1)
    sigma = jax.nn.sigmoid(gate_pre)
    hidden = (gate_pre * sigma * up_pre).astype(BF16)
    half = hidden.shape[0] // 2
    out_high = dot(hidden[half:], down, NN).astype(BF16)
    out_low = dot(hidden[:half], down, NN).astype(BF16)
    out_total = total_x(out_low, out_high)
    out_blocks = join_y(out_total)

    pre_gate = (hidden_grad * up_pre * sigma * (1.0 + gate_pre * (1.0 - sigma))).astype(BF16)
    pre_up = (hidden_grad * gate_pre * sigma).astype(BF16)
    own_pre = jnp.concatenate([pre_gate[:, :width], pre_up[:, :width]], axis=1)
    par_pre = jnp.concatenate([pre_gate[:, width:], pre_up[:, width:]], axis=1)
    back_high = (dot(own_pre[half:], own_gu, NT) + dot(par_pre[half:], par_gu, NT)).astype(BF16)
    back_low = (dot(own_pre[:half], own_gu, NT) + dot(par_pre[:half], par_gu, NT)).astype(BF16)
    back_total = total_x(back_low, back_high)

    send_down = dot(hidden[:, width:], cot_in, TN).astype(BF16)
    own_down = dot(hidden[:, :width], cot_in, TN)
    got_down = swap_w(send_down)
    grad_down = (own_down + got_down.astype(F32)).astype(BF16)
    got_gu = swap_w(dot(rows_in, par_pre, TN).astype(BF16))
    own_grad = dot(rows_in, own_pre, TN)
    grad_gu = (own_grad + got_gu.astype(F32)).astype(BF16)
    grad_gate = grad_gu[:, :width]
    grad_up = grad_gu[:, width:]

    expert_out = back_z(out_blocks)
    expert_back = back_z(join_y(back_total))

    layer_out = jnp.dot(weighted, expert_out.astype(F32), precision=lax.Precision.HIGHEST).astype(BF16)
    products = dot(cotangent, expert_out, NT)
    gate_part = jnp.sum(placed * products[:, None, :], axis=2)
    gate_grad = gate_part + swap_n(gate_part)
    gate_mean = jnp.sum(gate_share * gate_grad, axis=1, keepdims=True)
    logit_grad = jnp.sum(picked * (gate_share * (gate_grad - gate_mean))[:, :, None], axis=1).astype(BF16)
    router_back = dot(logit_grad, router_weight, NT)
    input_grad = (dot(occupied, expert_back, NN) + router_back).astype(BF16)
    return (layer_out, input_grad, grad_gate, grad_up, grad_down)


def solution(mesh):
    return jax.shard_map(
        local,
        mesh=mesh,
        in_specs=(
            P("wide", "narrow"),
            P("narrow", None),
            P("wide", None),
            P("wide", None),
            P("narrow", "wide"),
            P("narrow", "wide"),
            P("wide", "narrow"),
            P("wide", "narrow"),
        ),
        out_specs=(
            P("wide", "narrow"),
            P("wide", "narrow"),
            P("narrow", "wide"),
            P("narrow", "wide"),
            P("wide", "narrow"),
        ),
        check_vma=False,
    )
```

```python
import jax
import jax.numpy as jnp
import numpy as np
from jax import lax
from jax.experimental import pallas as pl
from jax.experimental.pallas import tpu as pltpu
from jax.sharding import PartitionSpec as P

CAP = 12
NZ, NYH, NX, NC = 8, 2, 4, 2
BLOCK = 2 * CAP
F32 = jnp.float32
BF16 = jnp.bfloat16


def wide_perm(move):
    pairs = []
    for z in range(NZ):
        for y in range(NYH):
            for x in range(NX):
                for c in range(NC):
                    a, b, d, e = move(z, y, x, c)
                    pairs.append((((z * NYH + y) * NX + x) * NC + c, ((a * NYH + b) * NX + d) * NC + e))
    return pairs


PERM_C = wide_perm(lambda z, y, x, c: (z, y, x, 1 - c))
PERM_X = wide_perm(lambda z, y, x, c: (z, y, x ^ 1, c))
PAIRS = [
    [((z * NYH + y) * NX + x) * NC + c for x in pair]
    for z in range(NZ)
    for y in range(NYH)
    for c in range(NC)
    for pair in ((0, 3), (1, 2))
]
PERM_W = wide_perm(lambda z, y, x, c: (z, y, NX - 1 - x, c))
PERM_Y = wide_perm(lambda z, y, x, c: (z, 1 - y, x, c))
PERM_Z = [wide_perm(lambda z, y, x, c, k=k: ((z + k) % NZ, y, x, c)) for k in range(NZ)]
FAR_FIRST = (4, 3, 5, 2, 6, 1, 7)


def swap_c(v):
    return lax.ppermute(v, "wide", PERM_C)


def swap_x(v):
    return lax.ppermute(v, "wide", PERM_X)


def swap_w(v):
    return lax.ppermute(v, "wide", PERM_W)


def swap_y(v):
    return lax.ppermute(v, "wide", PERM_Y)


def swap_n(v):
    return lax.ppermute(v, "narrow", [(0, 1), (1, 0)])


def dot(a, b, dims, out=F32):
    return lax.dot_general(a, b, (dims, ((), ())), preferred_element_type=out)


NN = ((1,), (0,))
NT = ((1,), (1,))
TN = ((0,), (0,))


VMEM = pl.BlockSpec(memory_space=pltpu.VMEM)
ANY = pl.BlockSpec(memory_space=pl.ANY)
PARAMS = pltpu.CompilerParams(vmem_limit_bytes=16 * 2**20)


def merge(pieces, after=()):
    count = len(pieces)
    rows = [p.shape[0] for p in pieces]
    starts = [sum(rows[:i]) for i in range(count)]

    def kernel(*refs):
        out = refs[-1]
        for i in range(count):
            out[pl.ds(starts[i], rows[i]), :] = refs[i][...]

    return pl.pallas_call(
        kernel,
        out_shape=jax.ShapeDtypeStruct((sum(rows),) + pieces[0].shape[1:], pieces[0].dtype),
        in_specs=[VMEM] * count + [ANY] * len(after),
        out_specs=VMEM,
        compiler_params=PARAMS,
    )(*pieces, *after)


def merge_pair(own, partner, half):
    rows = own.shape[0]

    def kernel(half_ref, own_ref, partner_ref, out_ref):
        mine = pl.multiple_of(half_ref[0] * rows, rows)
        other = pl.multiple_of((1 - half_ref[0]) * rows, rows)
        out_ref[pl.ds(mine, rows), :] = own_ref[...]
        out_ref[pl.ds(other, rows), :] = partner_ref[...]

    return pl.pallas_call(
        kernel,
        out_shape=jax.ShapeDtypeStruct((2 * rows, own.shape[1]), own.dtype),
        in_specs=[pl.BlockSpec(memory_space=pltpu.SMEM), VMEM, VMEM],
        out_specs=VMEM,
        compiler_params=PARAMS,
    )(half.reshape(1), own, partner)


def by_half(arrays):
    rows = arrays[0].shape[0] // 2
    count = len(arrays)

    def kernel(*refs):
        for i in range(2 * count):
            refs[-1][pl.ds(i * rows, rows), :] = refs[i % count][pl.ds(i // count * rows, rows), :]

    return pl.pallas_call(
        kernel,
        out_shape=jax.ShapeDtypeStruct((2 * count * rows, arrays[0].shape[1]), arrays[0].dtype),
        in_specs=[VMEM] * count,
        out_specs=VMEM,
        compiler_params=PARAMS,
    )(*arrays)


def reorder(pieces, order, sizes, after=()):
    count = len(pieces)
    starts = [sum(sizes[:i]) for i in range(len(sizes))]
    select = jnp.asarray(order[:, None] == np.arange(len(order))[None, :], BF16)

    def kernel(select_ref, *refs):
        ins, outs = refs[:count], refs[count + len(after) :]
        rows = jnp.concatenate([r[...].astype(F32) for r in ins], axis=0).astype(BF16)
        for start, out in zip(starts, outs):
            picked = dot(select_ref[pl.ds(start, out.shape[0]), :], rows, NN)
            out[...] = picked.astype(BF16)

    return pl.pallas_call(
        kernel,
        out_shape=[jax.ShapeDtypeStruct((size, pieces[0].shape[1]), BF16) for size in sizes],
        in_specs=[VMEM] * (1 + count) + [ANY] * len(after),
        out_specs=[VMEM] * len(sizes),
        compiler_params=PARAMS,
    )(select, *pieces, *after)


ROW = np.arange(NZ * CAP)
SPLIT = np.concatenate([ROW // CAP * BLOCK + ROW % CAP, ROW // CAP * BLOCK + ROW % CAP + CAP])
JOIN = np.argsort(SPLIT)


def one_hot(column_ref, weight_ref=None):
    slot = lax.broadcasted_iota(jnp.int32, (NZ * BLOCK, column_ref.shape[1]), 0)
    total = jnp.zeros(slot.shape, F32)
    for k in range(column_ref.shape[0]):
        value = 1.0 if weight_ref is None else weight_ref[k : k + 1, :]
        total = total + jnp.where(slot == column_ref[k : k + 1, :], value, 0.0)
    return total


def pack_rows(column, tokens, router_weight):
    def kernel(column_ref, tokens_ref, router_ref, *outs):
        rows = dot(one_hot(column_ref).astype(BF16), tokens_ref[...], NN)
        for k in range(NZ):
            outs[k][...] = rows[k * BLOCK : (k + 1) * BLOCK].astype(BF16)
        outs[NZ][...] = dot(tokens_ref[...], router_ref[...], NN)

    out = pl.pallas_call(
        kernel,
        out_shape=[jax.ShapeDtypeStruct((BLOCK, tokens.shape[1]), BF16)] * NZ
        + [jax.ShapeDtypeStruct((tokens.shape[0], router_weight.shape[1]), F32)],
        in_specs=[VMEM] * 3,
        out_specs=[VMEM] * (NZ + 1),
        compiler_params=PARAMS,
    )(column, tokens, router_weight)
    return out[:NZ], out[NZ]


def pack_cot(column, share, cotangent, after):
    def kernel(column_ref, share_ref, cot_ref, *refs):
        outs = refs[len(after) :]
        scale = jnp.sum(one_hot(column_ref, share_ref), axis=1, keepdims=True)
        rows = dot(one_hot(column_ref).astype(BF16), cot_ref[...], NN) * scale
        for k in range(NZ):
            outs[k][...] = rows[k * BLOCK : (k + 1) * BLOCK].astype(BF16)

    return pl.pallas_call(
        kernel,
        out_shape=[jax.ShapeDtypeStruct((BLOCK, cotangent.shape[1]), BF16)] * NZ,
        in_specs=[VMEM] * 3 + [ANY] * len(after),
        out_specs=[VMEM] * NZ,
        compiler_params=PARAMS,
    )(column, share, cotangent, *after)


def stack(blocks, after=()):
    count = len(blocks)

    def kernel(*refs):
        refs[-1][...] = jnp.concatenate([r[...].astype(F32) for r in refs[:count]], axis=0).astype(BF16)

    return pl.pallas_call(
        kernel,
        out_shape=jax.ShapeDtypeStruct((count * BLOCK, blocks[0].shape[1]), BF16),
        in_specs=[VMEM] * count + [ANY] * len(after),
        out_specs=VMEM,
        compiler_params=PARAMS,
    )(*blocks, *after)


def along_z(blocks):
    got = [blocks[0]] + [None] * (NZ - 1)
    for k in FAR_FIRST:
        got[k] = lax.ppermute(blocks[k], "wide", PERM_Z[k])
    return got


def split_y(got, after=()):
    return reorder(got, SPLIT, [NZ * CAP] * 2, after)


def spread(part, after=()):
    mine = merge([part, swap_x(part)])
    return merge([mine, swap_c(mine)], after)


def add_c(low, high):
    both = low.astype(F32) + swap_c(high).astype(F32)
    half = low.shape[0] // 2
    return both[:half], both[half:].astype(BF16)


def add_x(mine, sent):
    return (mine + swap_x(sent).astype(F32)).astype(BF16)


def join_y(keep, other, after=()):
    return reorder([keep, other], JOIN, [BLOCK] * NZ, after)


def back_z(blocks):
    got = [blocks[0]] + [None] * (NZ - 1)
    for k in FAR_FIRST:
        got[k] = lax.ppermute(blocks[k], "wide", PERM_Z[NZ - k])
    return got


def local(tokens, router_weight, route_ids, slot_index, w_gate, w_up, w_down, cotangent):
    width = w_gate.shape[1]
    place = lax.axis_index("wide")
    my_z = place // (NYH * NX * NC)
    my_y = (place // (NX * NC)) % NYH
    my_x = (place // NC) % NX

    def of_pair(value):
        return lax.all_gather(value, "wide", axis_index_groups=PAIRS, tiled=True)

    gate_t, up_t = w_gate.T, w_up.T
    gate_w = merge_pair(gate_t, swap_w(gate_t), (my_x >= NX // 2).astype(jnp.int32))
    up_w = of_pair(up_t)
    pair_down = of_pair(w_down)

    slots = NZ * BLOCK
    shift = (route_ids // NYH - my_z) % NZ
    flip = (route_ids % NYH) ^ my_y
    column = jnp.where(route_ids < NZ * NYH, shift * BLOCK + flip * CAP + slot_index, -1)
    slot_iota = lax.broadcasted_iota(jnp.int32, (1, 1, slots), 2)
    placed = (column[:, :, None] == slot_iota).astype(F32)
    occupied = jnp.sum(placed, axis=1).astype(BF16)
    send_rows, logits_part = pack_rows(column.T, tokens, router_weight)
    logits = logits_part + swap_n(logits_part)
    expert_iota = lax.broadcasted_iota(jnp.int32, (1, 1, router_weight.shape[1]), 2)
    picked = (route_ids[:, :, None] == expert_iota).astype(F32)
    chosen = jnp.sum(picked * logits[:, None, :], axis=2)
    weights_exp = jnp.exp(chosen)
    gate_share = weights_exp / jnp.sum(weights_exp, axis=1, keepdims=True)
    weighted = jnp.sum(placed * gate_share[:, :, None], axis=1)
    keep, give = split_y(along_z(send_rows), after=(gate_share,))
    other = swap_y(give)

    def gate_up(rows):
        parts = [dot(rows, w, NT) for w in (gate_w, up_w)]
        sents = [p.astype(BF16) for p in parts]
        return parts, sents, [swap_n(p) for p in sents]

    rows_a = spread(keep)
    rows_b = spread(other)
    parts_a, sents_a, gots_a = gate_up(rows_a)
    parts_b, sents_b, gots_b = gate_up(rows_b)
    send_cot = pack_cot(column.T, gate_share.T, cotangent, after=[keep])
    cot_keep, cot_give = split_y(along_z(send_cot), after=sents_a)
    cot_other = swap_y(cot_give)
    down = merge([pair_down], after=(cot_keep,))

    def forward(parts, gots):
        gate, up = [p + q.astype(F32) for p, q in zip(parts, gots)]
        sigma = jax.nn.sigmoid(gate)
        hidden = (gate * sigma * up).astype(BF16)
        half = hidden.shape[0] // 2
        high = dot(hidden[half:], down, NN).astype(BF16)
        low = dot(hidden[:half], down, NN).astype(BF16)
        return gate, up, sigma, hidden, high, low

    def backward(gate, up, sigma, grad):
        pre_gate = (grad * up * sigma * (1.0 + gate * (1.0 - sigma))).astype(BF16)
        pre_up = (grad * gate * sigma).astype(BF16)
        half = grad.shape[0] // 2
        high = (dot(pre_gate[half:], gate_w, NN) + dot(pre_up[half:], up_w, NN)).astype(BF16)
        low = (dot(pre_gate[:half], gate_w, NN) + dot(pre_up[:half], up_w, NN)).astype(BF16)
        return pre_gate, pre_up, high, low

    gate_a, up_a, sigma_a, hidden_a, high_a, low_a = forward(parts_a, gots_a)
    gate_b, up_b, sigma_b, hidden_b, high_b, low_b = forward(parts_b, gots_b)
    outs = (high_a, low_a, high_b, low_b)
    out_a = add_x(*add_c(low_a, high_a))
    out_b = add_x(*add_c(low_b, high_b))
    out_other = swap_y(out_b)
    cot_a = spread(cot_keep, after=outs)
    cot_b = spread(cot_other, after=outs)

    part_a = dot(cot_a, down, NT)
    part_b = dot(cot_b, down, NT)
    sents = (part_a.astype(BF16), part_b.astype(BF16))
    hg_a = part_a + swap_n(sents[0]).astype(F32)
    hg_b = part_b + swap_n(sents[1]).astype(F32)
    cot_all = merge([cot_a, cot_b], after=sents)
    part_down = dot(jnp.concatenate([hidden_a, hidden_b], axis=0), cot_all, TN).astype(BF16)

    pre_gate_a, pre_up_a, high_a, low_a = backward(gate_a, up_a, sigma_a, hg_a)
    pre_gate_b, pre_up_b, high_b, low_b = backward(gate_b, up_b, sigma_b, hg_b)
    backs = (high_a, low_a, high_b, low_b)
    mine_a, sent_a = add_c(low_a, high_a)
    mine_b, sent_b = add_c(low_b, high_b)
    out_blocks = join_y(out_a, out_other, after=(sent_a, sent_b))
    back_a = add_x(mine_a, sent_a)
    back_b = add_x(mine_b, sent_b)

    rows_all = merge([rows_a, rows_b], after=backs + (out_a, out_b))
    pairs = ((pre_gate_a, pre_gate_b), (pre_up_a, pre_up_b))
    grads = by_half([dot(jnp.concatenate(pair, axis=0), rows_all, TN).astype(BF16) for pair in pairs] + [part_down])
    other_back = swap_y(back_b)
    back_blocks = join_y(back_a, other_back, after=(grads,))
    grads = lax.psum_scatter(grads, "wide", axis_index_groups=PAIRS, scatter_dimension=0, tiled=True)
    grad_gate = grads[:width].T
    grad_up = grads[width : 2 * width].T
    grad_down = grads[2 * width :]

    expert_out = stack(back_z(out_blocks), after=(other_back,))
    expert_back = stack(back_z(back_blocks))

    layer_out = jnp.dot(weighted, expert_out.astype(F32), precision=lax.Precision.HIGHEST).astype(BF16)
    products = dot(cotangent, expert_out, NT)
    gate_part = jnp.sum(placed * products[:, None, :], axis=2)
    gate_grad = gate_part + swap_n(gate_part)
    gate_mean = jnp.sum(gate_share * gate_grad, axis=1, keepdims=True)
    logit_grad = jnp.sum(picked * (gate_share * (gate_grad - gate_mean))[:, :, None], axis=1).astype(BF16)
    router_back = dot(logit_grad, router_weight, NT)
    input_grad = (dot(occupied, expert_back, NN) + router_back).astype(BF16)
    return (layer_out, input_grad, grad_gate, grad_up, grad_down)


def solution(mesh):
    return jax.shard_map(
        local,
        mesh=mesh,
        in_specs=(
            P("wide", "narrow"),
            P("narrow", None),
            P("wide", None),
            P("wide", None),
            P("narrow", "wide"),
            P("narrow", "wide"),
            P("wide", "narrow"),
            P("wide", "narrow"),
        ),
        out_specs=(
            P("wide", "narrow"),
            P("wide", "narrow"),
            P("narrow", "wide"),
            P("narrow", "wide"),
            P("wide", "narrow"),
        ),
        check_vma=False,
    )
```

```python
import jax
import jax.numpy as jnp
import numpy as np
from jax import lax
from jax.experimental import pallas as pl
from jax.experimental.pallas import tpu as pltpu
from jax.sharding import PartitionSpec as P

CAP = 12
NZ, NYH, NX, NC = 8, 2, 4, 2
BLOCK = 2 * CAP
F32 = jnp.float32
BF16 = jnp.bfloat16


def wide_perm(move):
    pairs = []
    for z in range(NZ):
        for y in range(NYH):
            for x in range(NX):
                for c in range(NC):
                    a, b, d, e = move(z, y, x, c)
                    pairs.append((((z * NYH + y) * NX + x) * NC + c, ((a * NYH + b) * NX + d) * NC + e))
    return pairs


PERM_C = wide_perm(lambda z, y, x, c: (z, y, x, 1 - c))
PERM_X = wide_perm(lambda z, y, x, c: (z, y, x ^ 1, c))
PAIRS = [
    [((z * NYH + y) * NX + x) * NC + c for x in pair]
    for z in range(NZ)
    for y in range(NYH)
    for c in range(NC)
    for pair in ((0, 3), (1, 2))
]
PERM_Y = wide_perm(lambda z, y, x, c: (z, 1 - y, x, c))
PERM_Z = [wide_perm(lambda z, y, x, c, k=k: ((z + k) % NZ, y, x, c)) for k in range(NZ)]
FAR_FIRST = (4, 3, 5, 2, 6, 1, 7)


def swap_c(v):
    return lax.ppermute(v, "wide", PERM_C)


def swap_x(v):
    return lax.ppermute(v, "wide", PERM_X)


def swap_y(v):
    return lax.ppermute(v, "wide", PERM_Y)


def swap_n(v):
    return lax.ppermute(v, "narrow", [(0, 1), (1, 0)])


def dot(a, b, dims, out=F32):
    return lax.dot_general(a, b, (dims, ((), ())), preferred_element_type=out)


NN = ((1,), (0,))
NT = ((1,), (1,))
TN = ((0,), (0,))


VMEM = pl.BlockSpec(memory_space=pltpu.VMEM)
ANY = pl.BlockSpec(memory_space=pl.ANY)
PARAMS = pltpu.CompilerParams(vmem_limit_bytes=16 * 2**20)


def merge(pieces, after=()):
    count = len(pieces)
    rows = [p.shape[0] for p in pieces]
    starts = [sum(rows[:i]) for i in range(count)]

    def kernel(*refs):
        out = refs[-1]
        for i in range(count):
            out[pl.ds(starts[i], rows[i]), :] = refs[i][...]

    return pl.pallas_call(
        kernel,
        out_shape=jax.ShapeDtypeStruct((sum(rows),) + pieces[0].shape[1:], pieces[0].dtype),
        in_specs=[VMEM] * count + [ANY] * len(after),
        out_specs=VMEM,
        compiler_params=PARAMS,
    )(*pieces, *after)


def from_half(both):
    rows = both.shape[0] // 4

    def kernel(both_ref, *outs):
        for i in range(4):
            outs[i % 2][pl.ds(i // 2 * rows, rows), :] = both_ref[pl.ds(i * rows, rows), :]

    return pl.pallas_call(
        kernel,
        out_shape=[jax.ShapeDtypeStruct((2 * rows, both.shape[1]), both.dtype)] * 2,
        in_specs=[VMEM],
        out_specs=[VMEM] * 2,
        compiler_params=PARAMS,
    )(both)


def by_half(arrays, after=()):
    rows = arrays[0].shape[0] // 2
    count = len(arrays)

    def kernel(*refs):
        for i in range(2 * count):
            refs[-1][pl.ds(i * rows, rows), :] = refs[i % count][pl.ds(i // count * rows, rows), :]

    return pl.pallas_call(
        kernel,
        out_shape=jax.ShapeDtypeStruct((2 * count * rows, arrays[0].shape[1]), arrays[0].dtype),
        in_specs=[VMEM] * count + [ANY] * len(after),
        out_specs=VMEM,
        compiler_params=PARAMS,
    )(*arrays, *after)


def reorder(pieces, order, sizes, after=()):
    count = len(pieces)
    starts = [sum(sizes[:i]) for i in range(len(sizes))]
    select = jnp.asarray(order[:, None] == np.arange(len(order))[None, :], BF16)

    def kernel(select_ref, *refs):
        ins, outs = refs[:count], refs[count + len(after) :]
        rows = jnp.concatenate([r[...].astype(F32) for r in ins], axis=0).astype(BF16)
        for start, out in zip(starts, outs):
            picked = dot(select_ref[pl.ds(start, out.shape[0]), :], rows, NN)
            out[...] = picked.astype(BF16)

    return pl.pallas_call(
        kernel,
        out_shape=[jax.ShapeDtypeStruct((size, pieces[0].shape[1]), BF16) for size in sizes],
        in_specs=[VMEM] * (1 + count) + [ANY] * len(after),
        out_specs=[VMEM] * len(sizes),
        compiler_params=PARAMS,
    )(select, *pieces, *after)


ROW = np.arange(NZ * CAP)
SPLIT = np.concatenate([ROW // CAP * BLOCK + ROW % CAP, ROW // CAP * BLOCK + ROW % CAP + CAP])
JOIN = np.argsort(SPLIT)


def one_hot(column_ref, weight_ref=None):
    slot = lax.broadcasted_iota(jnp.int32, (NZ * BLOCK, column_ref.shape[1]), 0)
    total = jnp.zeros(slot.shape, F32)
    for k in range(column_ref.shape[0]):
        value = 1.0 if weight_ref is None else weight_ref[k : k + 1, :]
        total = total + jnp.where(slot == column_ref[k : k + 1, :], value, 0.0)
    return total


def pack_rows(column, tokens, router_weight):
    def kernel(column_ref, tokens_ref, router_ref, *outs):
        rows = dot(one_hot(column_ref).astype(BF16), tokens_ref[...], NN)
        for k in range(NZ):
            outs[k][...] = rows[k * BLOCK : (k + 1) * BLOCK].astype(BF16)
        outs[NZ][...] = dot(tokens_ref[...], router_ref[...], NN)

    out = pl.pallas_call(
        kernel,
        out_shape=[jax.ShapeDtypeStruct((BLOCK, tokens.shape[1]), BF16)] * NZ
        + [jax.ShapeDtypeStruct((tokens.shape[0], router_weight.shape[1]), F32)],
        in_specs=[VMEM] * 3,
        out_specs=[VMEM] * (NZ + 1),
        compiler_params=PARAMS,
    )(column, tokens, router_weight)
    return out[:NZ], out[NZ]


def pack_cot(column, share, cotangent, after):
    def kernel(column_ref, share_ref, cot_ref, *refs):
        outs = refs[len(after) :]
        scale = jnp.sum(one_hot(column_ref, share_ref), axis=1, keepdims=True)
        rows = dot(one_hot(column_ref).astype(BF16), cot_ref[...], NN) * scale
        for k in range(NZ):
            outs[k][...] = rows[k * BLOCK : (k + 1) * BLOCK].astype(BF16)

    return pl.pallas_call(
        kernel,
        out_shape=[jax.ShapeDtypeStruct((BLOCK, cotangent.shape[1]), BF16)] * NZ,
        in_specs=[VMEM] * 3 + [ANY] * len(after),
        out_specs=[VMEM] * NZ,
        compiler_params=PARAMS,
    )(column, share, cotangent, *after)


def stack(blocks, after=()):
    count = len(blocks)

    def kernel(*refs):
        refs[-1][...] = jnp.concatenate([r[...].astype(F32) for r in refs[:count]], axis=0).astype(BF16)

    return pl.pallas_call(
        kernel,
        out_shape=jax.ShapeDtypeStruct((count * BLOCK, blocks[0].shape[1]), BF16),
        in_specs=[VMEM] * count + [ANY] * len(after),
        out_specs=VMEM,
        compiler_params=PARAMS,
    )(*blocks, *after)


def along_z(blocks):
    got = [blocks[0]] + [None] * (NZ - 1)
    for k in FAR_FIRST:
        got[k] = lax.ppermute(blocks[k], "wide", PERM_Z[k])
    return got


def split_y(got, after=()):
    return reorder(got, SPLIT, [NZ * CAP] * 2, after)


def with_near(part, after=()):
    return merge([part, swap_x(part)], after)


def with_core(mine, after=()):
    return merge([mine, swap_c(mine)], after)


def add_c(low, high):
    both = low.astype(F32) + swap_c(high).astype(F32)
    half = low.shape[0] // 2
    return both[:half], both[half:].astype(BF16)


def add_x(mine, sent):
    return (mine + swap_x(sent).astype(F32)).astype(BF16)


def join_y(keep, other, after=()):
    return reorder([keep, other], JOIN, [BLOCK] * NZ, after)


def back_z(blocks):
    got = [blocks[0]] + [None] * (NZ - 1)
    for k in FAR_FIRST:
        got[k] = lax.ppermute(blocks[k], "wide", PERM_Z[NZ - k])
    return got


def local(tokens, router_weight, route_ids, slot_index, w_gate, w_up, w_down, cotangent):
    width = w_gate.shape[1]
    place = lax.axis_index("wide")
    my_z = place // (NYH * NX * NC)
    my_y = (place // (NX * NC)) % NYH

    def of_pair(value):
        return lax.all_gather(value, "wide", axis_index_groups=PAIRS, tiled=True)

    gate_w, up_w = from_half(of_pair(merge([w_gate.T, w_up.T])))
    pair_down = of_pair(w_down)

    slots = NZ * BLOCK
    shift = (route_ids // NYH - my_z) % NZ
    flip = (route_ids % NYH) ^ my_y
    column = jnp.where(route_ids < NZ * NYH, shift * BLOCK + flip * CAP + slot_index, -1)
    slot_iota = lax.broadcasted_iota(jnp.int32, (1, 1, slots), 2)
    placed = (column[:, :, None] == slot_iota).astype(F32)
    occupied = jnp.sum(placed, axis=1).astype(BF16)
    send_rows, logits_part = pack_rows(column.T, tokens, router_weight)
    logits = logits_part + swap_n(logits_part)
    expert_iota = lax.broadcasted_iota(jnp.int32, (1, 1, router_weight.shape[1]), 2)
    picked = (route_ids[:, :, None] == expert_iota).astype(F32)
    chosen = jnp.sum(picked * logits[:, None, :], axis=2)
    weights_exp = jnp.exp(chosen)
    gate_share = weights_exp / jnp.sum(weights_exp, axis=1, keepdims=True)
    weighted = jnp.sum(placed * gate_share[:, :, None], axis=1)
    keep, give = split_y(along_z(send_rows), after=(gate_share,))
    other = swap_y(give)

    def gate_up(rows):
        parts = [dot(rows, w, NT) for w in (gate_w, up_w)]
        sents = [p.astype(BF16) for p in parts]
        return parts, sents, [swap_n(p) for p in sents]

    got_cot = along_z(pack_cot(column.T, gate_share.T, cotangent, after=[keep]))
    rows_a = with_core(with_near(keep, after=got_cot[1:3]))
    rows_b = with_core(with_near(other, after=got_cot[3:6]))
    parts_a, sents_a, gots_a = gate_up(rows_a)
    parts_b, sents_b, gots_b = gate_up(rows_b)
    cot_keep, cot_give = split_y(got_cot, after=sents_a)
    cot_near_a = with_near(cot_keep)
    cot_near_b = with_near(swap_y(cot_give))
    gots_b = [merge([got], after=(cot_near_a, cot_near_b)) for got in gots_b]
    down = merge([pair_down], after=(cot_keep,))

    def forward(parts, gots):
        gate, up = [p + q.astype(F32) for p, q in zip(parts, gots)]
        sigma = jax.nn.sigmoid(gate)
        hidden = (gate * sigma * up).astype(BF16)
        half = hidden.shape[0] // 2
        high = dot(hidden[half:], down, NN).astype(BF16)
        low = dot(hidden[:half], down, NN).astype(BF16)
        return gate, up, sigma, hidden, high, low

    def backward(gate, up, sigma, grad):
        pre_gate = (grad * up * sigma * (1.0 + gate * (1.0 - sigma))).astype(BF16)
        pre_up = (grad * gate * sigma).astype(BF16)
        half = grad.shape[0] // 2
        high = (dot(pre_gate[half:], gate_w, NN) + dot(pre_up[half:], up_w, NN)).astype(BF16)
        low = (dot(pre_gate[:half], gate_w, NN) + dot(pre_up[:half], up_w, NN)).astype(BF16)
        return pre_gate, pre_up, high, low

    gate_a, up_a, sigma_a, hidden_a, high_a, low_a = forward(parts_a, gots_a)
    gate_b, up_b, sigma_b, hidden_b, high_b, low_b = forward(parts_b, gots_b)
    outs = (high_a, low_a, high_b, low_b)
    out_a = add_x(*add_c(low_a, high_a))
    out_b = add_x(*add_c(low_b, high_b))
    out_other = swap_y(out_b)
    cot_a = with_core(cot_near_a, after=outs)
    cot_b = with_core(cot_near_b, after=outs)

    part_a = dot(cot_a, down, NT)
    part_b = dot(cot_b, down, NT)
    sents = (part_a.astype(BF16), part_b.astype(BF16))
    hg_a = part_a + swap_n(sents[0]).astype(F32)
    hg_b = part_b + swap_n(sents[1]).astype(F32)
    cot_all = merge([cot_a, cot_b], after=sents)
    part_down = dot(jnp.concatenate([hidden_a, hidden_b], axis=0), cot_all, TN).astype(BF16)

    pre_gate_a, pre_up_a, high_a, low_a = backward(gate_a, up_a, sigma_a, hg_a)
    pre_gate_b, pre_up_b, high_b, low_b = backward(gate_b, up_b, sigma_b, hg_b)
    backs = (high_a, low_a, high_b, low_b)
    mine_a, sent_a = add_c(low_a, high_a)
    mine_b, sent_b = add_c(low_b, high_b)
    out_blocks = join_y(out_a, out_other, after=(sent_a, sent_b))
    back_a = add_x(mine_a, sent_a)
    back_b = add_x(mine_b, sent_b)

    rows_all = merge([rows_a, rows_b], after=backs + (out_a, out_b))
    pairs = ((pre_gate_a, pre_gate_b), (pre_up_a, pre_up_b))
    grads = by_half([dot(jnp.concatenate(pair, axis=0), rows_all, TN).astype(BF16) for pair in pairs] + [part_down], after=(out_other, sent_a, sent_b))
    other_back = swap_y(back_b)
    back_blocks = join_y(back_a, other_back, after=(grads,))
    grads = lax.psum_scatter(grads, "wide", axis_index_groups=PAIRS, scatter_dimension=0, tiled=True)
    grad_gate = grads[:width].T
    grad_up = grads[width : 2 * width].T
    grad_down = grads[2 * width :]

    expert_out = stack(back_z(out_blocks), after=(other_back,))
    expert_back = stack(back_z(back_blocks))

    layer_out = jnp.dot(weighted, expert_out.astype(F32), precision=lax.Precision.HIGHEST).astype(BF16)
    products = dot(cotangent, expert_out, NT)
    gate_part = jnp.sum(placed * products[:, None, :], axis=2)
    gate_grad = gate_part + swap_n(gate_part)
    gate_mean = jnp.sum(gate_share * gate_grad, axis=1, keepdims=True)
    logit_grad = jnp.sum(picked * (gate_share * (gate_grad - gate_mean))[:, :, None], axis=1).astype(BF16)
    router_back = dot(logit_grad, router_weight, NT)
    input_grad = (dot(occupied, expert_back, NN) + router_back).astype(BF16)
    return (layer_out, input_grad, grad_gate, grad_up, grad_down)


def solution(mesh):
    return jax.shard_map(
        local,
        mesh=mesh,
        in_specs=(
            P("wide", "narrow"),
            P("narrow", None),
            P("wide", None),
            P("wide", None),
            P("narrow", "wide"),
            P("narrow", "wide"),
            P("wide", "narrow"),
            P("wide", "narrow"),
        ),
        out_specs=(
            P("wide", "narrow"),
            P("wide", "narrow"),
            P("narrow", "wide"),
            P("narrow", "wide"),
            P("wide", "narrow"),
        ),
        check_vma=False,
    )
```

```python
import jax
import jax.numpy as jnp
import numpy as np
from jax import lax
from jax.experimental import pallas as pl
from jax.experimental.pallas import tpu as pltpu
from jax.sharding import PartitionSpec as P

CAP = 12
NZ, NYH, NX, NC = 8, 2, 4, 2
BLOCK = 2 * CAP
F32 = jnp.float32
BF16 = jnp.bfloat16


def wide_perm(move):
    pairs = []
    for z in range(NZ):
        for y in range(NYH):
            for x in range(NX):
                for c in range(NC):
                    a, b, d, e = move(z, y, x, c)
                    pairs.append((((z * NYH + y) * NX + x) * NC + c, ((a * NYH + b) * NX + d) * NC + e))
    return pairs


PERM_C = wide_perm(lambda z, y, x, c: (z, y, x, 1 - c))
PERM_X = wide_perm(lambda z, y, x, c: (z, y, x ^ 1, c))
PAIRS = [
    [((z * NYH + y) * NX + x) * NC + c for x in pair]
    for z in range(NZ)
    for y in range(NYH)
    for c in range(NC)
    for pair in ((0, 3), (1, 2))
]
PERM_Y = wide_perm(lambda z, y, x, c: (z, 1 - y, x, c))
PERM_Z = [wide_perm(lambda z, y, x, c, k=k: ((z + k) % NZ, y, x, c)) for k in range(NZ)]
FAR_FIRST = (4, 3, 5, 2, 6, 1, 7)


def swap_c(v):
    return lax.ppermute(v, "wide", PERM_C)


def swap_x(v):
    return lax.ppermute(v, "wide", PERM_X)


def swap_y(v):
    return lax.ppermute(v, "wide", PERM_Y)


def swap_n(v):
    return lax.ppermute(v, "narrow", [(0, 1), (1, 0)])


def dot(a, b, dims, out=F32):
    return lax.dot_general(a, b, (dims, ((), ())), preferred_element_type=out)


NN = ((1,), (0,))
NT = ((1,), (1,))
TN = ((0,), (0,))


VMEM = pl.BlockSpec(memory_space=pltpu.VMEM)
ANY = pl.BlockSpec(memory_space=pl.ANY)
PARAMS = pltpu.CompilerParams(vmem_limit_bytes=16 * 2**20)


def merge(pieces, after=()):
    count = len(pieces)
    rows = [p.shape[0] for p in pieces]
    starts = [sum(rows[:i]) for i in range(count)]

    def kernel(*refs):
        out = refs[-1]
        for i in range(count):
            out[pl.ds(starts[i], rows[i]), :] = refs[i][...]

    return pl.pallas_call(
        kernel,
        out_shape=jax.ShapeDtypeStruct((sum(rows),) + pieces[0].shape[1:], pieces[0].dtype),
        in_specs=[VMEM] * count + [ANY] * len(after),
        out_specs=VMEM,
        compiler_params=PARAMS,
    )(*pieces, *after)


def from_half(both, count):
    rows = both.shape[0] // (2 * count)

    def kernel(both_ref, *outs):
        for i in range(2 * count):
            outs[i % count][pl.ds(i // count * rows, rows), :] = both_ref[pl.ds(i * rows, rows), :]

    return pl.pallas_call(
        kernel,
        out_shape=[jax.ShapeDtypeStruct((2 * rows, both.shape[1]), both.dtype)] * count,
        in_specs=[VMEM],
        out_specs=[VMEM] * count,
        compiler_params=PARAMS,
    )(both)


def by_half(arrays, after=()):
    rows = arrays[0].shape[0] // 2
    count = len(arrays)

    def kernel(*refs):
        for i in range(2 * count):
            refs[-1][pl.ds(i * rows, rows), :] = refs[i % count][pl.ds(i // count * rows, rows), :]

    return pl.pallas_call(
        kernel,
        out_shape=jax.ShapeDtypeStruct((2 * count * rows, arrays[0].shape[1]), arrays[0].dtype),
        in_specs=[VMEM] * count + [ANY] * len(after),
        out_specs=VMEM,
        compiler_params=PARAMS,
    )(*arrays, *after)


def reorder(pieces, order, sizes, after=()):
    count = len(pieces)
    starts = [sum(sizes[:i]) for i in range(len(sizes))]
    select = jnp.asarray(order[:, None] == np.arange(len(order))[None, :], BF16)

    def kernel(select_ref, *refs):
        ins, outs = refs[:count], refs[count + len(after) :]
        rows = jnp.concatenate([r[...].astype(F32) for r in ins], axis=0).astype(BF16)
        for start, out in zip(starts, outs):
            picked = dot(select_ref[pl.ds(start, out.shape[0]), :], rows, NN)
            out[...] = picked.astype(BF16)

    return pl.pallas_call(
        kernel,
        out_shape=[jax.ShapeDtypeStruct((size, pieces[0].shape[1]), BF16) for size in sizes],
        in_specs=[VMEM] * (1 + count) + [ANY] * len(after),
        out_specs=[VMEM] * len(sizes),
        compiler_params=PARAMS,
    )(select, *pieces, *after)


ROW = np.arange(NZ * CAP)
SPLIT = np.concatenate([ROW // CAP * BLOCK + ROW % CAP, ROW // CAP * BLOCK + ROW % CAP + CAP])
JOIN = np.argsort(SPLIT)


def one_hot(column_ref, weight_ref=None):
    slot = lax.broadcasted_iota(jnp.int32, (NZ * BLOCK, column_ref.shape[1]), 0)
    total = jnp.zeros(slot.shape, F32)
    for k in range(column_ref.shape[0]):
        value = 1.0 if weight_ref is None else weight_ref[k : k + 1, :]
        total = total + jnp.where(slot == column_ref[k : k + 1, :], value, 0.0)
    return total


def pack_rows(column, tokens, router_weight):
    def kernel(column_ref, tokens_ref, router_ref, *outs):
        rows = dot(one_hot(column_ref).astype(BF16), tokens_ref[...], NN)
        for k in range(NZ):
            outs[k][...] = rows[k * BLOCK : (k + 1) * BLOCK].astype(BF16)
        outs[NZ][...] = dot(tokens_ref[...], router_ref[...], NN)

    out = pl.pallas_call(
        kernel,
        out_shape=[jax.ShapeDtypeStruct((BLOCK, tokens.shape[1]), BF16)] * NZ
        + [jax.ShapeDtypeStruct((tokens.shape[0], router_weight.shape[1]), F32)],
        in_specs=[VMEM] * 3,
        out_specs=[VMEM] * (NZ + 1),
        compiler_params=PARAMS,
    )(column, tokens, router_weight)
    return out[:NZ], out[NZ]


def pack_cot(column, share, cotangent, after):
    def kernel(column_ref, share_ref, cot_ref, *refs):
        outs = refs[len(after) :]
        scale = jnp.sum(one_hot(column_ref, share_ref), axis=1, keepdims=True)
        rows = dot(one_hot(column_ref).astype(BF16), cot_ref[...], NN) * scale
        for k in range(NZ):
            outs[k][...] = rows[k * BLOCK : (k + 1) * BLOCK].astype(BF16)

    return pl.pallas_call(
        kernel,
        out_shape=[jax.ShapeDtypeStruct((BLOCK, cotangent.shape[1]), BF16)] * NZ,
        in_specs=[VMEM] * 3 + [ANY] * len(after),
        out_specs=[VMEM] * NZ,
        compiler_params=PARAMS,
    )(column, share, cotangent, *after)


def stack(blocks, after=()):
    count = len(blocks)

    def kernel(*refs):
        refs[-1][...] = jnp.concatenate([r[...].astype(F32) for r in refs[:count]], axis=0).astype(BF16)

    return pl.pallas_call(
        kernel,
        out_shape=jax.ShapeDtypeStruct((count * BLOCK, blocks[0].shape[1]), BF16),
        in_specs=[VMEM] * count + [ANY] * len(after),
        out_specs=VMEM,
        compiler_params=PARAMS,
    )(*blocks, *after)


def along_z(blocks):
    got = [blocks[0]] + [None] * (NZ - 1)
    for k in FAR_FIRST:
        got[k] = lax.ppermute(blocks[k], "wide", PERM_Z[k])
    return got


def split_y(got, after=()):
    return reorder(got, SPLIT, [NZ * CAP] * 2, after)


def with_near(part, after=()):
    return merge([part, swap_x(part)], after)


def with_core(mine, after=()):
    return merge([mine, swap_c(mine)], after)


def add_c(low, high):
    both = low.astype(F32) + swap_c(high).astype(F32)
    half = low.shape[0] // 2
    return both[:half], both[half:].astype(BF16)


def add_x(mine, sent):
    return (mine + swap_x(sent).astype(F32)).astype(BF16)


def join_y(keep, other, after=()):
    return reorder([keep, other], JOIN, [BLOCK] * NZ, after)


def back_z(blocks):
    got = [blocks[0]] + [None] * (NZ - 1)
    for k in FAR_FIRST:
        got[k] = lax.ppermute(blocks[k], "wide", PERM_Z[NZ - k])
    return got


def local(tokens, router_weight, route_ids, slot_index, w_gate, w_up, w_down, cotangent):
    width = w_gate.shape[1]
    place = lax.axis_index("wide")
    my_z = place // (NYH * NX * NC)
    my_y = (place // (NX * NC)) % NYH

    weights = merge([w_gate.T, w_up.T, w_down])
    weights = lax.all_gather(weights, "wide", axis_index_groups=PAIRS, tiled=True)
    gate_w, up_w, pair_down = from_half(weights, 3)

    slots = NZ * BLOCK
    shift = (route_ids // NYH - my_z) % NZ
    flip = (route_ids % NYH) ^ my_y
    column = jnp.where(route_ids < NZ * NYH, shift * BLOCK + flip * CAP + slot_index, -1)
    slot_iota = lax.broadcasted_iota(jnp.int32, (1, 1, slots), 2)
    placed = (column[:, :, None] == slot_iota).astype(F32)
    occupied = jnp.sum(placed, axis=1).astype(BF16)
    send_rows, logits_part = pack_rows(column.T, tokens, router_weight)
    logits = logits_part + swap_n(logits_part)
    expert_iota = lax.broadcasted_iota(jnp.int32, (1, 1, router_weight.shape[1]), 2)
    picked = (route_ids[:, :, None] == expert_iota).astype(F32)
    chosen = jnp.sum(picked * logits[:, None, :], axis=2)
    weights_exp = jnp.exp(chosen)
    gate_share = weights_exp / jnp.sum(weights_exp, axis=1, keepdims=True)
    weighted = jnp.sum(placed * gate_share[:, :, None], axis=1)
    keep, give = split_y(along_z(send_rows), after=(gate_share,))
    other = swap_y(give)

    def gate_up(rows):
        parts = [dot(rows, w, NT) for w in (gate_w, up_w)]
        sents = [p.astype(BF16) for p in parts]
        return parts, sents, [swap_n(p) for p in sents]

    got_cot = along_z(pack_cot(column.T, gate_share.T, cotangent, after=[keep]))
    rows_a = with_core(with_near(keep, after=got_cot[1:2]))
    rows_b = with_core(with_near(other, after=got_cot[2:5]))
    parts_a, sents_a, gots_a = gate_up(rows_a)
    parts_b, sents_b, gots_b = gate_up(rows_b)
    cot_keep, cot_give = split_y(got_cot, after=sents_a)
    cot_near_a = with_near(cot_keep)
    cot_near_b = with_near(swap_y(cot_give))
    gots_b = [merge([got], after=(cot_near_a, cot_near_b)) for got in gots_b]
    down = merge([pair_down], after=(cot_keep,))

    def forward(parts, gots):
        gate, up = [p + q.astype(F32) for p, q in zip(parts, gots)]
        sigma = jax.nn.sigmoid(gate)
        hidden = (gate * sigma * up).astype(BF16)
        half = hidden.shape[0] // 2
        high = dot(hidden[half:], down, NN).astype(BF16)
        low = dot(hidden[:half], down, NN).astype(BF16)
        return gate, up, sigma, hidden, high, low

    def backward(gate, up, sigma, grad):
        pre_gate = (grad * up * sigma * (1.0 + gate * (1.0 - sigma))).astype(BF16)
        pre_up = (grad * gate * sigma).astype(BF16)
        half = grad.shape[0] // 2
        high = (dot(pre_gate[half:], gate_w, NN) + dot(pre_up[half:], up_w, NN)).astype(BF16)
        low = (dot(pre_gate[:half], gate_w, NN) + dot(pre_up[:half], up_w, NN)).astype(BF16)
        return pre_gate, pre_up, high, low

    gate_a, up_a, sigma_a, hidden_a, high_a, low_a = forward(parts_a, gots_a)
    gate_b, up_b, sigma_b, hidden_b, high_b, low_b = forward(parts_b, gots_b)
    outs = (high_a, low_a, high_b, low_b)
    out_a = add_x(*add_c(low_a, high_a))
    out_b = add_x(*add_c(low_b, high_b))
    out_other = swap_y(out_b)
    cot_a = with_core(cot_near_a, after=outs)
    cot_b = with_core(cot_near_b, after=outs)

    part_a = dot(cot_a, down, NT)
    part_b = dot(cot_b, down, NT)
    sents = (part_a.astype(BF16), part_b.astype(BF16))
    hg_a = part_a + swap_n(sents[0]).astype(F32)
    hg_b = part_b + swap_n(sents[1]).astype(F32)
    cot_all = merge([cot_a, cot_b], after=sents)
    part_down = dot(jnp.concatenate([hidden_a, hidden_b], axis=0), cot_all, TN).astype(BF16)

    pre_gate_a, pre_up_a, high_a, low_a = backward(gate_a, up_a, sigma_a, hg_a)
    pre_gate_b, pre_up_b, high_b, low_b = backward(gate_b, up_b, sigma_b, hg_b)
    backs = (high_a, low_a, high_b, low_b)
    mine_a, sent_a = add_c(low_a, high_a)
    mine_b, sent_b = add_c(low_b, high_b)
    out_blocks = join_y(out_a, out_other, after=(sent_a, sent_b))
    back_a = add_x(mine_a, sent_a)
    back_b = add_x(mine_b, sent_b)

    rows_all = merge([rows_a, rows_b], after=backs + (out_a, out_b))
    pairs = ((pre_gate_a, pre_gate_b), (pre_up_a, pre_up_b))
    grads = by_half([dot(jnp.concatenate(pair, axis=0), rows_all, TN).astype(BF16) for pair in pairs] + [part_down], after=(out_other, sent_a, sent_b))
    other_back = swap_y(back_b)
    back_blocks = join_y(back_a, other_back, after=(grads,))
    grads = lax.psum_scatter(grads, "wide", axis_index_groups=PAIRS, scatter_dimension=0, tiled=True)
    grad_gate = grads[:width].T
    grad_up = grads[width : 2 * width].T
    grad_down = grads[2 * width :]

    expert_out = stack(back_z(out_blocks), after=(other_back,))
    expert_back = stack(back_z(back_blocks))

    layer_out = jnp.dot(weighted, expert_out.astype(F32), precision=lax.Precision.HIGHEST).astype(BF16)
    products = dot(cotangent, expert_out, NT)
    gate_part = jnp.sum(placed * products[:, None, :], axis=2)
    gate_grad = gate_part + swap_n(gate_part)
    gate_mean = jnp.sum(gate_share * gate_grad, axis=1, keepdims=True)
    logit_grad = jnp.sum(picked * (gate_share * (gate_grad - gate_mean))[:, :, None], axis=1).astype(BF16)
    router_back = dot(logit_grad, router_weight, NT)
    input_grad = (dot(occupied, expert_back, NN) + router_back).astype(BF16)
    return (layer_out, input_grad, grad_gate, grad_up, grad_down)


def solution(mesh):
    return jax.shard_map(
        local,
        mesh=mesh,
        in_specs=(
            P("wide", "narrow"),
            P("narrow", None),
            P("wide", None),
            P("wide", None),
            P("narrow", "wide"),
            P("narrow", "wide"),
            P("wide", "narrow"),
            P("wide", "narrow"),
        ),
        out_specs=(
            P("wide", "narrow"),
            P("wide", "narrow"),
            P("narrow", "wide"),
            P("narrow", "wide"),
            P("wide", "narrow"),
        ),
        check_vma=False,
    )
```
